256 devices in a mesh: reader: 128 (over z, x_lo, y, core), segment: 2 (over x_hi).
Axes of the slice: x: 4 (x_hi: 2, x_lo: 2; x = x_hi * 2 + x_lo), y: 4, z: 8, core: 2. Of those that a mesh axis runs over, the one named last changes fastest.
Arguments:
- dec_input: bfloat16 [2048, 16, 16, 512], P('reader'), may hold values from -6 to 6
- out_cotangent: bfloat16 [2048, 16, 16, 512], P('reader'), may hold values from -6 to 6
- pooled_skip: bfloat16 [2048, 8, 8, 256], P('reader'), may hold values from -6 to 6
- deep_input: bfloat16 [2048, 8, 8, 512], P('reader'), may hold values from -6 to 6
- dec_weight: bfloat16 [9, 64, 64], replicated, may hold values from -0.25 to 0.25
- deep_weight: bfloat16 [27, 128, 128], replicated, may hold values from -0.109375 to 0.109375
- up_weight: bfloat16 [128, 64], replicated, may hold values from -0.5 to 0.5
- down_weight: bfloat16 [64, 128], replicated, may hold values from -0.75 to 0.75
- counts: int32 [128], replicated, may hold values from 2 to 16, as said below
Outputs:
- skip_grad: bfloat16 [2048, 16, 16, 512], P('reader', 'segment')
- dec_weight_grad: float32 [9, 64, 64], replicated
- deep_weight_grad: float32 [27, 128, 128], replicated
- up_weight_grad: float32 [128, 64], replicated
- down_weight_grad: float32 [64, 128], replicated
The draws below stay inside these ranges and needn't reach their ends.
Inputs may be any that keep to these rules, and one draw needn't show every extreme that they name: `counts`: each reader holds between 2 and 16 occupied blocks, in its first slots; some reader holds 16 and some holds 2.
All inputs are finite; a program needn't handle non-finite values.
Results may differ from the reference program's by a relative error of at most 0.0069.
Values may be sent and summed in bfloat16 or wider, within the bound.
No kernel may reach another device: no remote copies, remote signals or barrier semaphores. Data moves between devices by JAX's collectives and lax.ppermute only.
A program may use at most 128 MiB of HBM per device.

```python
import math
import jax
import jax.numpy as jnp
from jax import lax

C0 = 64
C1 = 128
BX = 16
BY = 16
BZ = 8
MAXB = 16
SLOTS = 2048
N_READER = 128


def draw_counts(key, part):
    key_level = jax.random.fold_in(key, 11)
    key_high = jax.random.fold_in(key, 12)
    key_low = jax.random.fold_in(key, 13)
    level = jax.random.randint(key_level, (N_READER,), 0, 64, dtype=jnp.int32)
    counts = 2 + level * level * level * (MAXB - 1) // 262144
    high_pos = jax.random.randint(key_high, (), 0, N_READER, dtype=jnp.int32)
    low_pos = (high_pos + 1 + jax.random.randint(key_low, (), 0, N_READER - 1, dtype=jnp.int32)) % N_READER
    counts = counts.at[high_pos].set(MAXB)
    counts = counts.at[low_pos].set(2)
    return counts.astype(jnp.int32)


def levels(rng, extent, cuts, least, top_value):
    def one(axis_at, parts):
        draws = jax.random.uniform(jax.random.fold_in(jax.random.fold_in(rng, 6), axis_at), (parts,), jnp.float32, least / len(cuts), top_value / len(cuts))
        return jnp.repeat(jnp.exp(draws), extent[axis_at] // parts).reshape((-1,) + (1,) * (len(extent) - axis_at - 1))

    gain = one(*cuts[0])
    for cut in cuts[1:]:
        gain = gain * one(*cut)
    return gain


def centred(rng, shape, scale, reach, shards=(), kind=jnp.bfloat16):
    level = levels(rng, shape, shards, -0.22, 0.18) if shards else 1.0
    values = jax.random.normal(rng, shape, jnp.float32) * scale * level
    return jnp.minimum(jnp.maximum(values, -reach), reach).astype(kind)


def setup_inputs(seed: int = 0) -> dict:
    key_of = jax.random.split(jax.random.key(seed), 10)
    return {
        "dec_input": centred(key_of[0], (SLOTS, BX, BY, BZ * C0), 1.0, 6.0, ((0, 128),)),
        "out_cotangent": centred(key_of[1], (SLOTS, BX, BY, BZ * C0), 1.0, 6.0, ((0, 128),)),
        "pooled_skip": centred(key_of[2], (SLOTS, BX // 2, BY // 2, (BZ // 2) * C0), 1.0, 6.0, ((0, 128),)),
        "deep_input": centred(key_of[3], (SLOTS, BX // 2, BY // 2, (BZ // 2) * C1), 1.0, 6.0, ((0, 128),)),
        "dec_weight": centred(key_of[4], (9, C0, C0), (9 * C0) ** -0.5, 0.25),
        "deep_weight": centred(key_of[5], (27, C1, C1), (27 * C1) ** -0.5, 0.109375),
        "up_weight": centred(key_of[6], (C1, C0), C1 ** -0.5, 0.5),
        "down_weight": centred(key_of[7], (C0, C1), C0 ** -0.5, 0.75),
        "counts": draw_counts(jax.random.fold_in(key_of[9], 71), 0),
    }


TAPS_FLAT = [(shift_x, shift_y, 0) for shift_x in (-1, 0, 1) for shift_y in (-1, 0, 1)]
TAPS_CUBE = [(shift_x, shift_y, shift_z) for shift_x in (-1, 0, 1) for shift_y in (-1, 0, 1) for shift_z in (-1, 0, 1)]

def gather_taps(volume, tap_list, direction):
    width_x, width_y, width_z = (volume.shape[0], volume.shape[1], volume.shape[2])
    padded = jnp.pad(volume, ((1, 1), (1, 1), (1, 1), (0, 0)))
    pieces = [padded[1 + direction * shift_x:1 + direction * shift_x + width_x, 1 + direction * shift_y:1 + direction * shift_y + width_y, 1 + direction * shift_z:1 + direction * shift_z + width_z] for shift_x, shift_y, shift_z in tap_list]
    return jnp.concatenate(pieces, axis=-1)

def apply_taps(volume, matrix, tap_list, direction):
    stacked = gather_taps(volume, tap_list, direction)
    flattened = stacked.reshape(-1, stacked.shape[-1])
    result = jnp.dot(flattened, matrix, preferred_element_type=jnp.float32)
    return result.reshape(volume.shape[:3] + (matrix.shape[1],))

def weight_taps(volume, gradient, tap_list):
    stacked = gather_taps(volume, tap_list, 1)
    flattened = stacked.reshape(-1, stacked.shape[-1])
    return jnp.dot(flattened.T, gradient.reshape(-1, gradient.shape[-1]), preferred_element_type=jnp.float32)

def shallow_block(out_block, grad_block, dec_back):
    volume = out_block.reshape(BX, BY, BZ, C0)
    upstream = grad_block.reshape(BX, BY, BZ, C0)
    rectified = jnp.maximum(volume, jnp.zeros_like(volume))
    weight_part = weight_taps(rectified, upstream, TAPS_FLAT)
    backed = apply_taps(upstream, dec_back, TAPS_FLAT, -1)
    skip_total = (upstream.astype(jnp.float32) + jnp.where(volume > 0, backed, jnp.float32(0.0))).astype(jnp.bfloat16)
    coarse = skip_total.astype(jnp.float32).reshape(BX // 2, 2, BY // 2, 2, BZ // 2, 2, C0).sum(axis=(1, 3, 5)).astype(jnp.bfloat16)
    return (skip_total.reshape(BX, BY, BZ * C0), coarse.reshape(BX // 2, BY // 2, BZ // 2 * C0), weight_part)

def deep_block(coarse_grad, pooled_block, saved_deep, deep_fwd, deep_back, up_back, down_back):
    upstream = coarse_grad.reshape(-1, C0)
    start_vol = saved_deep.reshape(BX // 2, BY // 2, BZ // 2, C1)
    rectified = jnp.maximum(start_vol, jnp.zeros_like(start_vol))
    deep_out = (start_vol.astype(jnp.float32) + apply_taps(rectified, deep_fwd, TAPS_CUBE, 1)).astype(jnp.bfloat16)
    up_part = jnp.dot(deep_out.reshape(-1, C1).T, upstream, preferred_element_type=jnp.float32)
    deep_grad = jnp.dot(upstream, up_back, preferred_element_type=jnp.float32).astype(jnp.bfloat16)
    deep_grad = deep_grad.reshape(BX // 2, BY // 2, BZ // 2, C1)
    deep_part = weight_taps(rectified, deep_grad, TAPS_CUBE)
    backed = apply_taps(deep_grad, deep_back, TAPS_CUBE, -1)
    input_grad = (deep_grad.astype(jnp.float32) + jnp.where(start_vol > 0, backed, jnp.float32(0.0))).astype(jnp.bfloat16)
    flat_input = input_grad.reshape(-1, C1)
    down_part = jnp.dot(pooled_block.reshape(-1, C0).T, flat_input, preferred_element_type=jnp.float32)
    pool_grad = jnp.dot(flat_input, down_back, preferred_element_type=jnp.float32).astype(jnp.bfloat16)
    return (pool_grad.reshape(BX // 2, BY // 2, BZ // 2 * C0), deep_part, up_part, down_part)

def expand_coarse(coarse):
    number = coarse.shape[0]
    rows_x = coarse.shape[1]
    spread_out = coarse.astype(jnp.float32).reshape(number, rows_x, 1, BY // 2, 1, BZ // 2, 1, C0)
    spread_out = jnp.broadcast_to(spread_out, (number, rows_x, 2, BY // 2, 2, BZ // 2, 2, C0))
    return spread_out.reshape(number, 2 * rows_x, BY, BZ * C0)

def finish(fine_half, coarse):
    return (fine_half.astype(jnp.float32) + 0.125 * expand_coarse(coarse)).astype(jnp.bfloat16)

def reference(dec_input, out_cotangent, pooled_skip, deep_input, dec_weight, deep_weight, up_weight, down_weight, counts):
    dec_back = dec_weight.transpose(0, 2, 1).reshape(9 * C0, C0)
    deep_fwd = deep_weight.reshape(27 * C1, C1)
    deep_back = deep_weight.transpose(0, 2, 1).reshape(27 * C1, C1)
    up_back = up_weight.T
    down_back = down_weight.T

    def visit_slot(totals, slot_id):
        is_valid = slot_id % MAXB < counts[slot_id // MAXB]

        def active(unused):
            skip_total, coarse, dec_part = shallow_block(dec_input[slot_id], out_cotangent[slot_id], dec_back)
            pool_grad, deep_part, up_part, down_part = deep_block(coarse, pooled_skip[slot_id], deep_input[slot_id], deep_fwd, deep_back, up_back, down_back)
            finished = finish(skip_total[None], pool_grad[None])[0]
            return (finished, dec_part, deep_part, up_part, down_part)

        def skipped(unused):
            return (jnp.zeros((BX, BY, BZ * C0), jnp.bfloat16), jnp.zeros((9 * C0, C0), jnp.float32), jnp.zeros((27 * C1, C1), jnp.float32), jnp.zeros((C1, C0), jnp.float32), jnp.zeros((C0, C1), jnp.float32))
        finished, dec_part, deep_part, up_part, down_part = lax.cond(is_valid, active, skipped, 0)
        totals = (totals[0] + dec_part, totals[1] + deep_part, totals[2] + up_part, totals[3] + down_part)
        return (totals, finished)
    initial = (jnp.zeros((9 * C0, C0), jnp.float32), jnp.zeros((27 * C1, C1), jnp.float32), jnp.zeros((C1, C0), jnp.float32), jnp.zeros((C0, C1), jnp.float32))
    slot_ids = jnp.arange(N_READER * MAXB, dtype=jnp.int32)
    totals, skip_grad = lax.scan(visit_slot, initial, slot_ids)
    grad_scale = 1.0 / math.sqrt(N_READER * MAXB * BX * BY * BZ)
    return (skip_grad, (totals[0] * grad_scale).reshape(9, C0, C0), (totals[1] * grad_scale).reshape(27, C1, C1), totals[2] * grad_scale, totals[3] * grad_scale)
```

```python
import functools
import math

import jax
import jax.numpy as jnp
from jax import lax
from jax.experimental import pallas as pl
from jax.experimental.pallas import tpu as pltpu
from jax.sharding import Mesh, PartitionSpec as P

C0 = 64
C1 = 128
BX = 16
BY = 16
BZ = 8
F32 = jnp.float32
BF16 = jnp.bfloat16
OFFS = (-1, 0, 1)


def cat(parts, axis):
    return parts[0] if len(parts) == 1 else jnp.concatenate(parts, axis=axis)


def lanes(index, width=128):
    return slice(index * width, (index + 1) * width)


def shift_rows(value, distance, keep):
    rows = value.shape[0]
    return jnp.where(keep, pltpu.roll(value, distance % rows, 0), F32(0.0))


def dot(lhs, rhs):
    return jnp.dot(lhs, rhs, preferred_element_type=F32)


def shallow_kernel(
    info_ref, grad_ref, out_ref, wpair_ref, skip_ref, coarse_ref, dec_ref,
    shifted, turned, toeplitz, spread, total,
):
    step = pl.program_id(0)
    half = info_ref[0]
    count = info_ref[1]
    sign = 1 - 2 * half

    @pl.when(step == 0)
    def _():
        for dyi in range(3):
            for b in range(2):
                shifted[dyi, b, 0] = jnp.zeros((BY, 512), BF16)
        turned[0] = jnp.zeros((128, 128), BF16)
        for w in range(4):
            for dyi in range(3):
                for xi in range(2):
                    dxf = 1 + xi - w
                    if abs(dxf) <= 1:
                        block = wpair_ref[3 * (dxf * sign + 1) + dyi]
                    else:
                        block = jnp.zeros((128, 128), BF16)
                    toeplitz[lanes(3 * w + dyi), lanes(xi)] = block
        total[...] = jnp.zeros_like(total)

    row_id = lax.broadcasted_iota(jnp.int32, (BY, 512), 0)
    not_first = row_id > 0
    not_last = row_id < BY - 1
    for b in range(2):
        live = 2 * step + b < count
        for i in range(11):
            value = grad_ref[b, half * 15 + sign * i].astype(F32)
            value = jnp.where(live, value, F32(0.0))
            shifted[0, b, i + 1] = shift_rows(value, -1, not_last).astype(BF16)
            shifted[1, b, i + 1] = value.astype(BF16)
            shifted[2, b, i + 1] = shift_rows(value, 1, not_first).astype(BF16)

    for i in range(9):
        parts = []
        for b in range(2):
            row = out_ref[b, half * 15 + sign * i]
            row = jnp.maximum(row, jnp.zeros_like(row))
            parts += [row[:, lanes(z)] for z in range(4)]
        turned[i + 1] = cat(parts, 0).T

    lhs = cat([cat([turned[i + dxi] for i in range(8)], 1) for dxi in range(3)], 0)
    rhs = cat(
        [
            cat([shifted[dyi, b, i + 1, :, lanes(z)] for dyi in range(3)], 1)
            for i in range(8)
            for b in range(2)
            for z in range(4)
        ],
        0,
    )
    total[...] += dot(lhs, rhs)

    lhs = cat(
        [
            cat(
                [
                    shifted[dyi, b, 2 * xp + w, :, lanes(z)]
                    for b in range(2)
                    for xp in range(5)
                    for z in range(4)
                ],
                0,
            )
            for w in range(4)
            for dyi in range(3)
        ],
        1,
    )
    backed = dot(lhs, toeplitz[...])
    low_lane = lax.broadcasted_iota(jnp.int32, (8, 128), 1) < 64
    for xp in range(5):
        pooled = []
        for b in range(2):
            both = []
            for xi in range(2):
                i = 2 * xp + xi
                base = (b * 5 + xp) * 64
                conv = cat([backed[base + 16 * z : base + 16 * z + 16, lanes(xi)] for z in range(4)], 1)
                gate = out_ref[b, half * 15 + sign * i].astype(F32) > 0
                value = shifted[1, b, i + 1].astype(F32) + jnp.where(gate, conv, F32(0.0))
                value = value.astype(BF16)
                if i < 8:
                    skip_ref[b, half * 7 + sign * i] = value
                both.append(value.astype(F32))
            cell = both[0] + both[1]
            cell = cat(
                [cell[:, lanes(z)] + pltpu.roll(cell[:, lanes(z)], 64, 1) for z in range(4)], 1
            )
            quads = []
            for z in range(4):
                spread[b, z] = cell[:, lanes(z)]
                even = spread[b, z, pl.ds(0, 8, stride=2), :]
                quads.append(even + spread[b, z, pl.ds(1, 8, stride=2), :])
            pooled.append(
                cat([jnp.where(low_lane, quads[2 * k], quads[2 * k + 1]) for k in range(2)], 1)
            )
        coarse_ref[xp] = cat(pooled, 0).astype(BF16)

    @pl.when(step == pl.num_programs(0) - 1)
    def _():
        low = lax.broadcasted_iota(jnp.int32, (64, 128), 1) < 64
        low_half = lax.broadcasted_iota(jnp.int32, (32, 128), 1) < 64
        for dxi in range(3):
            for dyi in range(3):
                block = total[lanes(dxi), lanes(dyi)]
                other = pltpu.roll(block, 64, 1)
                summed = jnp.where(low, block[:64] + other[64:], block[64:] + other[:64])
                tap = 3 * ((dxi - 1) * sign + 1) + dyi
                dec_ref[tap] = jnp.where(low_half, summed[:32], summed[32:])


def deep_kernel(
    info_ref, coarse_ref, pooled_ref, deep_ref, weight_ref, upt_ref, downt_ref,
    part_ref, upart_ref, dpart_ref, pool_grad_ref,
    start, rect, grads, pools, turned, wfwd, wback, up_mat, down_mat,
):
    half = info_ref[0]
    sign = 1 - 2 * half

    row_id = lax.broadcasted_iota(jnp.int32, (128, 512), 0) % 8
    not_first = row_id > 0
    not_last = row_id < 7

    for dyi in range(3):
        rect[dyi, 0] = jnp.zeros((128, 512), BF16)
        grads[dyi, 0] = jnp.zeros((128, 512), BF16)
    for z in range(4):
        turned[0, z] = jnp.zeros((128, 128), BF16)

    for i in range(5):
        source = half * 7 + sign * i
        for p in range(8):
            pair = cat([deep_ref[2 * p + b, source].astype(F32) for b in range(2)], 0)
            start[i, 16 * p : 16 * p + 16] = pair.astype(BF16)
            if i < 4:
                pair = cat([pooled_ref[2 * p + b, source].astype(F32) for b in range(2)], 0)
                pools[i, 16 * p : 16 * p + 16] = pair.astype(BF16)
        value = jnp.maximum(start[i].astype(F32), F32(0.0))
        rect[0, i + 1] = shift_rows(value, 1, not_first).astype(BF16)
        rect[1, i + 1] = value.astype(BF16)
        rect[2, i + 1] = shift_rows(value, -1, not_last).astype(BF16)
        for z in range(4):
            turned[i + 1, z] = rect[1, i + 1, :, lanes(z)].T

    zero = jnp.zeros((128, 128), BF16)
    for dxi in range(3):
        for dyi in range(3):
            tap = 9 * ((dxi - 1) * sign + 1) + 3 * dyi
            plain = [weight_ref[tap + k] for k in range(3)]
            flipped = [value.T for value in plain]
            for g in range(2):
                for zi in range(3):
                    for zo in range(2):
                        dz = (zi + g) - (zo + 2 * g)
                        rows = lanes((3 * dxi + dyi) * 3 + zi)
                        wfwd[g, rows, lanes(zo)] = plain[dz + 1] if abs(dz) <= 1 else zero
                        wback[g, rows, lanes(zo)] = flipped[1 - dz] if abs(dz) <= 1 else zero

    up_mat[...] = jnp.zeros_like(up_mat)
    down_mat[...] = jnp.zeros_like(down_mat)
    for z in range(4):
        up_mat[lanes(z, 64), lanes(z)] = upt_ref[...]
        down_mat[lanes(z), lanes(z)] = downt_ref[...]

    coarse = cat([coarse_ref[i] for i in range(5)], 0)
    grad = dot(coarse, up_mat[...])
    for i in range(5):
        value = grad[lanes(i)].astype(BF16).astype(F32)
        grads[0, i + 1] = shift_rows(value, -1, not_last).astype(BF16)
        grads[1, i + 1] = value.astype(BF16)
        grads[2, i + 1] = shift_rows(value, 1, not_first).astype(BF16)

    for dzi in range(3):
        dz = dzi - 1
        levels = [z for z in range(4) if 0 <= z + dz < 4]
        lhs = cat(
            [
                cat([turned[i + dxi, z + dz] for z in levels for i in range(4)], 1)
                for dxi in range(3)
            ],
            0,
        )
        rhs = cat(
            [
                cat([grads[dyi, i + 1, :, lanes(z)] for dyi in range(3)], 1)
                for z in levels
                for i in range(4)
            ],
            0,
        )
        part = dot(lhs, rhs)
        for dxi in range(3):
            for dyi in range(3):
                tap = 9 * ((dxi - 1) * sign + 1) + 3 * dyi + dzi
                part_ref[tap] = part[lanes(dxi), lanes(dyi)]

    outs = []
    for g in range(2):
        wide = slice(g * 128, g * 128 + 384)
        lhs = cat(
            [
                cat([rect[dyi, i + dxi, :, wide] for i in range(4)], 0)
                for dxi in range(3)
                for dyi in range(3)
            ],
            1,
        )
        conv = dot(lhs, wfwd[g])
        first = cat([start[i, :, lanes(g, 256)] for i in range(4)], 0).astype(F32)
        outs.append((first + conv).astype(BF16))
    coarse_t = cat([coarse_ref[i].T for i in range(4)], 1)
    full = dot(coarse_t, cat(outs, 1))
    upart_ref[...] = sum(full[lanes(z, 64), lanes(z)] for z in range(4))

    outs = []
    for g in range(2):
        wide = slice(g * 128, g * 128 + 384)
        lhs = cat(
            [
                cat([grads[dyi, i + 2 - dxi, :, wide] for i in range(4)], 0)
                for dxi in range(3)
                for dyi in range(3)
            ],
            1,
        )
        conv = dot(lhs, wback[g])
        first = cat([start[i, :, lanes(g, 256)] for i in range(4)], 0).astype(F32)
        base = cat([grads[1, i + 1, :, lanes(g, 256)] for i in range(4)], 0).astype(F32)
        outs.append((base + jnp.where(first > 0, conv, F32(0.0))).astype(BF16))
    input_grad = cat(outs, 1)
    pools_t = cat([pools[i].T for i in range(4)], 1)
    full = dot(pools_t, input_grad)
    dpart_ref[...] = sum(full[lanes(z, 64), lanes(z)] for z in range(4))
    pool_grad = dot(input_grad, down_mat[...]).astype(BF16)
    for i in range(4):
        pool_grad_ref[i] = pool_grad[lanes(i)]


def finish_kernel(info_ref, skip_ref, pool_ref, done_ref, spread):
    half = info_ref[0]
    sign = 1 - 2 * half
    for i in range(4):
        coarse = pool_ref[i].astype(F32) * F32(0.125)
        for b in range(2):
            value = coarse[8 * b : 8 * b + 8]
            for z in range(4):
                spread[b, z, pl.ds(0, 8, stride=2), :] = value[:, lanes(z)]
                spread[b, z, pl.ds(1, 8, stride=2), :] = value[:, lanes(z)]
            wide = cat([spread[b, z] for z in range(4)], 1)
            for xi in range(2):
                row = half * 7 + sign * (2 * i + xi)
                done_ref[b, row] = (skip_ref[b, row].astype(F32) + wide).astype(BF16)


def pair_blocks(weight):
    back = weight.transpose(0, 2, 1)
    zero = jnp.zeros_like(back)
    return jnp.concatenate(
        [jnp.concatenate([back, zero], 2), jnp.concatenate([zero, back], 2)], 1
    )


def local_work(half, count, dec_input, out_cotangent, pooled_skip, deep_input, dec_weight, deep_weight, up_weight, down_weight):
    info = jnp.stack([half, count]).astype(jnp.int32)
    slots = dec_input.shape[0]
    params = dict(vmem_limit_bytes=48 * 1024 * 1024)

    def whole(*shape):
        return pl.BlockSpec(shape, lambda s, info: (0,) * len(shape))

    fine = pl.BlockSpec((2, BX, BY, 512), lambda s, info: (s, 0, 0, 0))
    skip, coarse, dec_part = pl.pallas_call(
        shallow_kernel,
        grid_spec=pltpu.PrefetchScalarGridSpec(
            num_scalar_prefetch=1,
            grid=(slots // 2,),
            in_specs=[fine, fine, whole(9, 128, 128)],
            out_specs=[
                pl.BlockSpec((2, 8, BY, 512), lambda s, info: (s, 0, 0, 0)),
                pl.BlockSpec((5, 16, 256), lambda s, info: (0, s, 0)),
                whole(9, 32, 128),
            ],
            scratch_shapes=[
                pltpu.VMEM((3, 2, 12, BY, 512), BF16),
                pltpu.VMEM((10, 128, 128), BF16),
                pltpu.VMEM((1536, 256), BF16),
                pltpu.VMEM((2, 4, BY, 128), F32),
                pltpu.VMEM((384, 384), F32),
            ],
        ),
        out_shape=[
            jax.ShapeDtypeStruct((slots, 8, BY, 512), BF16),
            jax.ShapeDtypeStruct((5, slots * 8, 256), BF16),
            jax.ShapeDtypeStruct((9, 32, 128), F32),
        ],
        compiler_params=pltpu.CompilerParams(**params),
        name="shallow",
    )(info, out_cotangent, dec_input, pair_blocks(dec_weight))

    up_t = up_weight.T
    down_t = jnp.concatenate([down_weight.T, down_weight.T], 1)
    deep_part, up_part, down_part, pool_grad = pl.pallas_call(
        deep_kernel,
        grid_spec=pltpu.PrefetchScalarGridSpec(
            num_scalar_prefetch=1,
            grid=(1,),
            in_specs=[
                whole(5, 128, 256),
                whole(16, 8, 8, 256),
                whole(16, 8, 8, 512),
                whole(27, 128, 128),
                whole(64, 128),
                whole(128, 128),
            ],
            out_specs=[whole(27, 128, 128), whole(64, 128), whole(64, 128), whole(4, 128, 512)],
            scratch_shapes=[
                pltpu.VMEM((5, 128, 512), BF16),
                pltpu.VMEM((3, 6, 128, 512), BF16),
                pltpu.VMEM((3, 6, 128, 512), BF16),
                pltpu.VMEM((4, 128, 256), BF16),
                pltpu.VMEM((6, 4, 128, 128), BF16),
                pltpu.VMEM((2, 3456, 256), BF16),
                pltpu.VMEM((2, 3456, 256), BF16),
                pltpu.VMEM((256, 512), BF16),
                pltpu.VMEM((512, 512), BF16),
            ],
        ),
        out_shape=[
            jax.ShapeDtypeStruct((27, 128, 128), F32),
            jax.ShapeDtypeStruct((64, 128), F32),
            jax.ShapeDtypeStruct((64, 128), F32),
            jax.ShapeDtypeStruct((4, 128, 512), BF16),
        ],
        compiler_params=pltpu.CompilerParams(**params),
        name="deep",
    )(info, coarse, pooled_skip, deep_input, deep_weight, up_t, down_t)

    skip_grad = pl.pallas_call(
        finish_kernel,
        grid_spec=pltpu.PrefetchScalarGridSpec(
            num_scalar_prefetch=1,
            grid=(slots // 2,),
            in_specs=[
                pl.BlockSpec((2, 8, BY, 512), lambda s, info: (s, 0, 0, 0)),
                pl.BlockSpec((4, 16, 512), lambda s, info: (0, s, 0)),
            ],
            out_specs=pl.BlockSpec((2, 8, BY, 512), lambda s, info: (s, 0, 0, 0)),
            scratch_shapes=[pltpu.VMEM((2, 4, BY, 128), F32)],
        ),
        out_shape=jax.ShapeDtypeStruct((slots, 8, BY, 512), BF16),
        compiler_params=pltpu.CompilerParams(**params),
        name="finish",
    )(info, skip, pool_grad)
    return skip_grad, dec_part, deep_part, up_part, down_part


AXES = ("z", "xl", "y", "core", "xh")
READER = ("z", "xl", "y", "core")
PLANE = ("xl", "y", "xh")


def scatter_sum(rows, axes, parts):
    split = rows.reshape(parts, -1, 128)
    split = lax.all_to_all(split, axes, 0, 0, tiled=True)
    return split.sum(axis=0)


def gather(rows, axes, parts):
    copies = jnp.broadcast_to(rows[None], (parts,) + rows.shape)
    return lax.all_to_all(copies, axes, 0, 0, tiled=True).reshape(-1, 128)


def sum_everywhere(rows):
    core = lax.axis_index("core")
    swap = [(0, 1), (1, 0)]
    halves = rows.reshape(2, -1, 128)
    mine = lax.dynamic_index_in_dim(halves, core, 0, False)
    other = lax.dynamic_index_in_dim(halves, 1 - core, 0, False)
    mine = mine + lax.ppermute(other, "core", swap)
    mine = scatter_sum(mine, PLANE, 16)
    mine = scatter_sum(mine, "z", 8)
    mine = gather(mine.astype(BF16), "z", 8)
    mine = gather(mine, PLANE, 16)
    other = lax.ppermute(mine, "core", swap)
    low = jnp.where(core == 0, mine, other)
    high = jnp.where(core == 0, other, mine)
    return jnp.concatenate([low, high], axis=0).astype(F32)


def per_device(
    dec_input, out_cotangent, pooled_skip, deep_input,
    dec_weight, deep_weight, up_weight, down_weight, counts,
):
    reader = lax.axis_index(READER)
    half = lax.axis_index("xh")
    slots = dec_input.shape[0]
    skip_grad, dec_part, deep_part, up_part, down_part = local_work(
        half, counts[reader], dec_input, out_cotangent, pooled_skip, deep_input,
        dec_weight, deep_weight, up_weight, down_weight,
    )
    rows = jnp.concatenate(
        [deep_part.reshape(-1, 128), dec_part.reshape(-1, 128), up_part, down_part,
         jnp.zeros((224, 128), F32)], axis=0,
    )
    scale = 1.0 / math.sqrt(counts.shape[0] * slots * BX * BY * BZ)
    rows = sum_everywhere(rows) * scale
    deep_sum = rows[:3456].reshape(27, C1, C1)
    dec_sum = rows[3456:3744].reshape(9, 32, 128)
    dec_sum = jnp.concatenate([dec_sum[..., :64], dec_sum[..., 64:]], axis=1)
    up_sum = rows[3744:3808].T
    down_sum = rows[3808:3872]
    return skip_grad, dec_sum, deep_sum, up_sum, down_sum


def solution(mesh):
    fine = Mesh(mesh.devices.reshape(8, 2, 4, 2, 2), AXES)
    spec = P(READER, None, None, None)
    return jax.shard_map(
        per_device,
        mesh=fine,
        in_specs=(spec, spec, spec, spec, P(), P(), P(), P(), P()),
        out_specs=(P(READER, "xh", None, None), P(), P(), P(), P()),
        check_vma=False,
    )
```

```python
import math

import jax
import jax.numpy as jnp
from jax import lax
from jax.experimental import pallas as pl
from jax.experimental.pallas import tpu as pltpu
from jax.sharding import Mesh, PartitionSpec as P

C0 = 64
C1 = 128
BX = 16
BY = 16
BZ = 8
F32 = jnp.float32
BF16 = jnp.bfloat16

AXES = ("zh", "zl", "xl", "y", "core", "xh")
READER = ("zh", "zl", "xl", "y", "core")
NEAR = ("zl", "xl", "y", "xh")
FAR = "zh"
UNITS = 16


def cat(parts, axis):
    return parts[0] if len(parts) == 1 else jnp.concatenate(parts, axis=axis)


def lanes(index, width=128):
    return slice(index * width, (index + 1) * width)


def shift_rows(value, distance, keep):
    rows = value.shape[0]
    return jnp.where(keep, pltpu.roll(value, distance % rows, 0), F32(0.0))


def dot(lhs, rhs):
    return jnp.dot(lhs, rhs, preferred_element_type=F32)


def unit_of(dyi, dzi):
    first = 9 * dzi + 3 * dyi
    return (0, first) if first < 15 else (1, first - 15)


def work_kernel(
    counts_ref, grad_ref, out_ref, deep_ref, pooled_ref, wdec_ref, wdeep_ref, wup_ref, wdown_ref,
    skip_ref, pool_grad_ref, mine_ref, other_ref,
    shifted, turned, toeplitz, spread, total, tile, parts,
    start, rect, grads, pools, coarse, deep_turned, wfwd, wback, up_mat, down_mat, sems,
):
    step = pl.program_id(0)
    last = pl.num_programs(0) - 1
    half = lax.axis_index("xh")
    core = lax.axis_index("core")
    count = counts_ref[lax.axis_index(READER)]
    sign = 1 - 2 * half

    @pl.when(step == 0)
    def _():
        tile[...] = jnp.zeros_like(tile)
        low_lane = lax.broadcasted_iota(jnp.int32, (64, 128), 1) < 64
        backs = []
        for tap in range(9):
            tile[:64, :64] = wdec_ref[tap].astype(F32)
            upper = jnp.where(low_lane, tile[:64], F32(0.0))
            backs.append(cat([upper, pltpu.roll(upper, 64, 1)], 0).T.astype(BF16))
            turned_pair = backs[tap]
            parts[0, tap, :64] = turned_pair[:64].astype(F32)
            parts[0, tap, 64:] = turned_pair[64:].astype(F32)
        for w in range(4):
            for dyi in range(3):
                for xi in range(2):
                    dxf = 1 + xi - w
                    if abs(dxf) <= 1:
                        block = parts[0, 3 * (dxf * sign + 1) + dyi].astype(BF16)
                    else:
                        block = jnp.zeros((128, 128), BF16)
                    toeplitz[lanes(3 * w + dyi), lanes(xi)] = block
        total[...] = jnp.zeros_like(total)
        parts[1, UNITS - 1] = jnp.zeros((128, 128), F32)
        for dyi in range(3):
            for b in range(2):
                shifted[dyi, b, 0] = jnp.zeros((BY, 512), BF16)
            rect[dyi, 0] = jnp.zeros((128, 512), BF16)
            grads[dyi, 0] = jnp.zeros((128, 512), BF16)
        turned[0] = jnp.zeros((128, 128), BF16)
        for z in range(4):
            deep_turned[0, z] = jnp.zeros((128, 128), BF16)
        up_mat[...] = jnp.zeros_like(up_mat)
        down_mat[...] = jnp.zeros_like(down_mat)
        down = wdown_ref[...].astype(F32)
        down_t = cat([down, down], 0).T.astype(BF16)
        for z in range(4):
            up_mat[lanes(z, 64), lanes(z)] = wup_ref[...]
            down_mat[lanes(z), lanes(z)] = down_t

    def deep_weights():
        group = 3 * ((step // 3 - 1) * sign + 1) + step % 3
        zero = jnp.zeros((128, 128), BF16)
        plain = [wdeep_ref[k] for k in range(3)]
        flipped = [value.T for value in plain]
        for zi in range(3):
            rows = pl.ds(pl.multiple_of((group * 3 + zi) * 128, 128), 128)
            for g in range(2):
                for zo in range(2):
                    dz = (zi + g) - (zo + 2 * g)
                    wfwd[g, rows, lanes(zo)] = plain[dz + 1] if abs(dz) <= 1 else zero
                    wback[g, rows, lanes(zo)] = flipped[1 - dz] if abs(dz) <= 1 else zero

    @pl.when(step < last)
    def _():
        deep_weights()
        row_id = lax.broadcasted_iota(jnp.int32, (BY, 512), 0)
        not_first = row_id > 0
        not_last = row_id < BY - 1
        deep_first = row_id % 8 > 0
        deep_last = row_id % 8 < 7
        rows = pl.ds(pl.multiple_of(step * 16, 16), 16)
        for b in range(2):
            live = 2 * step + b < count
            for i in range(11):
                value = grad_ref[b, half * 15 + sign * i].astype(F32)
                value = jnp.where(live, value, F32(0.0))
                shifted[0, b, i + 1] = shift_rows(value, -1, not_last).astype(BF16)
                shifted[1, b, i + 1] = value.astype(BF16)
                shifted[2, b, i + 1] = shift_rows(value, 1, not_first).astype(BF16)
        for i in range(9):
            tiles = []
            for b in range(2):
                row = out_ref[b, half * 15 + sign * i]
                row = jnp.maximum(row, jnp.zeros_like(row))
                tiles += [row[:, lanes(z)] for z in range(4)]
            turned[i + 1] = cat(tiles, 0).T

        lhs = cat(
            [
                cat(
                    [
                        shifted[dyi, b, 2 * xp + w, :, lanes(z)]
                        for b in range(2)
                        for xp in range(5)
                        for z in range(4)
                    ],
                    0,
                )
                for w in range(4)
                for dyi in range(3)
            ],
            1,
        )
        backed = dot(lhs, toeplitz[...])

        lhs = cat([cat([turned[i + dxi] for i in range(8)], 1) for dxi in range(3)], 0)
        rhs = cat(
            [
                cat([shifted[dyi, b, i + 1, :, lanes(z)] for dyi in range(3)], 1)
                for i in range(8)
                for b in range(2)
                for z in range(4)
            ],
            0,
        )
        total[...] += dot(lhs, rhs)

        for i in range(5):
            source = half * 7 + sign * i
            value = cat([deep_ref[b, source].astype(F32) for b in range(2)], 0)
            start[i, rows] = value.astype(BF16)
            value = jnp.maximum(value, F32(0.0))
            rect[0, i + 1, rows] = shift_rows(value, 1, deep_first).astype(BF16)
            rect[1, i + 1, rows] = value.astype(BF16)
            rect[2, i + 1, rows] = shift_rows(value, -1, deep_last).astype(BF16)
            if i < 4:
                value = cat([pooled_ref[b, source].astype(F32) for b in range(2)], 0)
                pools[i, rows] = value.astype(BF16)

        low_lane = lax.broadcasted_iota(jnp.int32, (8, 128), 1) < 64
        for xp in range(5):
            pooled = []
            for b in range(2):
                both = []
                for xi in range(2):
                    i = 2 * xp + xi
                    base = (b * 5 + xp) * 64
                    conv = cat(
                        [backed[base + 16 * z : base + 16 * z + 16, lanes(xi)] for z in range(4)], 1
                    )
                    gate = out_ref[b, half * 15 + sign * i].astype(F32) > 0
                    value = shifted[1, b, i + 1].astype(F32) + jnp.where(gate, conv, F32(0.0))
                    value = value.astype(BF16)
                    if i < 8:
                        skip_ref[b, half * 7 + sign * i] = value
                    both.append(value.astype(F32))
                cell = both[0] + both[1]
                quads = []
                for z in range(4):
                    piece = cell[:, lanes(z)]
                    slot = (xp * 2 + b) * 4 + z
                    spread[slot] = piece + pltpu.roll(piece, 64, 1)
                    even = spread[slot, pl.ds(0, 8, stride=2), :]
                    quads.append(even + spread[slot, pl.ds(1, 8, stride=2), :])
                pooled.append(
                    cat(
                        [jnp.where(low_lane, quads[2 * k], quads[2 * k + 1]) for k in range(2)], 1
                    )
                )
            coarse[xp, rows] = cat(pooled, 0).astype(BF16)

    @pl.when(step == last)
    def _():
        deep_weights()
        row_id = lax.broadcasted_iota(jnp.int32, (128, 512), 0) % 8
        not_first = row_id > 0
        not_last = row_id < 7

        grad = dot(cat([coarse[i] for i in range(5)], 0), up_mat[...])
        for i in range(5):
            value = grad[lanes(i)].astype(BF16).astype(F32)
            grads[0, i + 1] = shift_rows(value, -1, not_last).astype(BF16)
            grads[1, i + 1] = value.astype(BF16)
            grads[2, i + 1] = shift_rows(value, 1, not_first).astype(BF16)
            for z in range(4):
                deep_turned[i + 1, z] = rect[1, i + 1, :, lanes(z)].T

        outs = []
        for g in range(2):
            wide = slice(g * 128, g * 128 + 384)
            lhs = cat(
                [
                    cat([rect[dyi, i + dxi, :, wide] for i in range(4)], 0)
                    for dxi in range(3)
                    for dyi in range(3)
                ],
                1,
            )
            conv = dot(lhs, wfwd[g])
            first = cat([start[i, :, lanes(g, 256)] for i in range(4)], 0).astype(F32)
            outs.append((first + conv).astype(BF16))
        coarse_t = cat([coarse[i].T for i in range(4)], 1)
        full = dot(coarse_t, cat(outs, 1))
        parts[0, UNITS - 1, :64] = sum(full[lanes(z, 64), lanes(z)] for z in range(4))

        for dzi in range(3):
            dz = dzi - 1
            levels = [z for z in range(4) if 0 <= z + dz < 4]
            lhs = cat(
                [
                    cat([deep_turned[i + dxi, z + dz] for z in levels for i in range(4)], 1)
                    for dxi in range(3)
                ],
                0,
            )
            rhs = cat(
                [
                    cat([grads[dyi, i + 1, :, lanes(z)] for dyi in range(3)], 1)
                    for z in levels
                    for i in range(4)
                ],
                0,
            )
            part = dot(lhs, rhs)
            for dyi in range(3):
                side, first = unit_of(dyi, dzi)
                for dxi in range(3):
                    parts[side, first + (dxi - 1) * sign + 1] = part[lanes(dxi), lanes(dyi)]

        low = lax.broadcasted_iota(jnp.int32, (64, 128), 1) < 64
        low_half = lax.broadcasted_iota(jnp.int32, (32, 128), 1) < 64
        for dxi in range(3):
            for dyi in range(3):
                block = total[lanes(dxi), lanes(dyi)]
                turned_lanes = pltpu.roll(block, 64, 1)
                summed = jnp.where(
                    low, block[:64] + turned_lanes[64:], block[64:] + turned_lanes[:64]
                )
                summed = jnp.where(low_half, summed[:32], summed[32:])
                row = pl.multiple_of(((dxi - 1) * sign + 1) * 32, 32)
                parts[1, 12 + dyi, pl.ds(row, 32)] = summed
        for dyi in range(3):
            parts[1, 12 + dyi, 96:] = jnp.zeros((32, 128), F32)

        outs = []
        for g in range(2):
            wide = slice(g * 128, g * 128 + 384)
            lhs = cat(
                [
                    cat([grads[dyi, i + 2 - dxi, :, wide] for i in range(4)], 0)
                    for dxi in range(3)
                    for dyi in range(3)
                ],
                1,
            )
            conv = dot(lhs, wback[g])
            first = cat([start[i, :, lanes(g, 256)] for i in range(4)], 0).astype(F32)
            base = cat([grads[1, i + 1, :, lanes(g, 256)] for i in range(4)], 0).astype(F32)
            outs.append((base + jnp.where(first > 0, conv, F32(0.0))).astype(BF16))
        input_grad = cat(outs, 1)
        full = dot(cat([pools[i].T for i in range(4)], 1), input_grad)
        parts[0, UNITS - 1, 64:] = sum(full[lanes(z, 64), lanes(z)] for z in range(4))
        send = pltpu.make_async_copy(parts.at[1 - core], other_ref, sems.at[0])
        keep = pltpu.make_async_copy(parts.at[core], mine_ref, sems.at[1])
        send.start()
        keep.start()
        pool_grad = dot(input_grad, down_mat[...]).astype(BF16)
        for i in range(4):
            pool_grad_ref[i] = pool_grad[lanes(i)]
        send.wait()
        keep.wait()


def finish_kernel(skip_ref, pool_ref, done_ref, spread):
    half = lax.axis_index("xh")
    sign = 1 - 2 * half
    for i in range(4):
        for p in range(2):
            coarse = pool_ref[i, 16 * p : 16 * p + 16].astype(F32) * F32(0.125)
            for b in range(2):
                value = coarse[8 * b : 8 * b + 8]
                wide = []
                for z in range(4):
                    slot = ((i * 2 + p) * 2 + b) * 4 + z
                    spread[slot, pl.ds(0, 8, stride=2), :] = value[:, lanes(z)]
                    spread[slot, pl.ds(1, 8, stride=2), :] = value[:, lanes(z)]
                    wide.append(spread[slot])
                wide = cat(wide, 1)
                for xi in range(2):
                    row = half * 7 + sign * (2 * i + xi)
                    value_in = skip_ref[2 * p + b, row].astype(F32)
                    done_ref[2 * p + b, row] = (value_in + wide).astype(BF16)


def unpack_kernel(mine_ref, other_ref, dec_ref, deep_ref, up_ref, down_ref, *, scale):
    first_half = lax.axis_index("core") == 0

    def unit(side, index):
        rows = lanes(index)
        mine = mine_ref[rows].astype(F32)
        other = other_ref[rows].astype(F32)
        return jnp.where(first_half, *((mine, other) if side == 0 else (other, mine))) * F32(scale)

    for dyi in range(3):
        for dzi in range(3):
            side, first = unit_of(dyi, dzi)
            for dxi in range(3):
                deep_ref[9 * dxi + 3 * dyi + dzi] = unit(side, first + dxi)
        block = unit(1, 12 + dyi)
        for dxi in range(3):
            piece = block[lanes(dxi, 32)]
            dec_ref[3 * dxi + dyi, :32] = piece[:, :64]
            dec_ref[3 * dxi + dyi, 32:] = pltpu.roll(piece, 64, 1)[:, :64]
    block = unit(0, UNITS - 1)
    up_ref[...] = block[:64]
    down_ref[...] = block[64:]


def whole(*shape):
    return pl.BlockSpec(shape, lambda *step: (0,) * len(shape))


def work(counts, dec_input, out_cotangent, pooled_skip, deep_input, dec_weight, deep_weight, up_weight, down_weight):
    slots = dec_input.shape[0]
    steps = slots // 2

    def pair(*shape):
        return pl.BlockSpec(
            (2,) + shape, lambda s, counts: (jnp.minimum(s, steps - 1),) + (0,) * len(shape)
        )

    anywhere = pl.BlockSpec(memory_space=pl.ANY)
    return pl.pallas_call(
        work_kernel,
        grid_spec=pltpu.PrefetchScalarGridSpec(
            num_scalar_prefetch=1,
            grid=(steps + 1,),
            in_specs=[
                pair(BX, BY, 512),
                pair(BX, BY, 512),
                pair(8, 8, 512),
                pair(8, 8, 256),
                whole(9, 64, 64),
                pl.BlockSpec((3, 128, 128), lambda s, counts: (s, 0, 0)),
                whole(64, 128),
                whole(64, 128),
            ],
            out_specs=[pair(8, BY, 512), whole(4, 8 * slots, 512), anywhere, anywhere],
            scratch_shapes=[
                pltpu.VMEM((3, 2, 12, BY, 512), BF16),
                pltpu.VMEM((10, 128, 128), BF16),
                pltpu.VMEM((1536, 256), BF16),
                pltpu.VMEM((40, BY, 128), F32),
                pltpu.VMEM((384, 384), F32),
                pltpu.VMEM((128, 128), F32),
                pltpu.VMEM((2, UNITS, 128, 128), F32),
                pltpu.VMEM((5, 128, 512), BF16),
                pltpu.VMEM((3, 6, 128, 512), BF16),
                pltpu.VMEM((3, 6, 128, 512), BF16),
                pltpu.VMEM((4, 128, 256), BF16),
                pltpu.VMEM((5, 128, 256), BF16),
                pltpu.VMEM((6, 4, 128, 128), BF16),
                pltpu.VMEM((2, 3456, 256), BF16),
                pltpu.VMEM((2, 3456, 256), BF16),
                pltpu.VMEM((256, 512), BF16),
                pltpu.VMEM((512, 512), BF16),
                pltpu.SemaphoreType.DMA((2,)),
            ],
        ),
        out_shape=[
            jax.ShapeDtypeStruct((slots, 8, BY, 512), BF16),
            jax.ShapeDtypeStruct((4, 8 * slots, 512), BF16),
            jax.ShapeDtypeStruct((UNITS, 128, 128), F32),
            jax.ShapeDtypeStruct((UNITS, 128, 128), F32),
        ],
        compiler_params=pltpu.CompilerParams(vmem_limit_bytes=60 * 1024 * 1024),
        name="work",
    )(counts, out_cotangent, dec_input, deep_input, pooled_skip, dec_weight, deep_weight, up_weight.T, down_weight)


def finish(skip, pool_grad):
    slots = skip.shape[0]
    blocks = pl.BlockSpec((4, 8, BY, 512), lambda s: (s, 0, 0, 0))
    return pl.pallas_call(
        finish_kernel,
        grid=(slots // 4,),
        in_specs=[blocks, pl.BlockSpec((4, 32, 512), lambda s: (0, s, 0))],
        out_specs=blocks,
        scratch_shapes=[pltpu.VMEM((64, BY, 128), F32)],
        out_shape=jax.ShapeDtypeStruct(skip.shape, BF16),
        compiler_params=pltpu.CompilerParams(vmem_limit_bytes=12 * 1024 * 1024),
        cost_estimate=pl.CostEstimate(flops=1 << 20, bytes_accessed=1 << 23, transcendentals=0),
        name="finish",
    )(skip, pool_grad)


def scatter_sum(rows, axes):
    split = rows.reshape(lax.axis_size(axes), -1, 128)
    split = lax.all_to_all(split, axes, 0, 0, tiled=True)
    return split.astype(F32).sum(axis=0)


def spread_out(rows, axes):
    copies = jnp.broadcast_to(rows[None], (lax.axis_size(axes),) + rows.shape)
    return lax.all_to_all(copies, axes, 0, 0, tiled=True)


def per_device(
    dec_input, out_cotangent, pooled_skip, deep_input,
    dec_weight, deep_weight, up_weight, down_weight, counts,
):
    slots = dec_input.shape[0]
    swap = [(0, 1), (1, 0)]
    skip, pool_grad, mine, other = work(
        counts, dec_input, out_cotangent, pooled_skip, deep_input,
        dec_weight, deep_weight, up_weight, down_weight,
    )
    other = lax.ppermute(other, "core", swap)
    rows = (mine + other).astype(BF16).reshape(-1, 128)
    rows = scatter_sum(rows, NEAR)
    rows = spread_out(rows, FAR).sum(axis=0).astype(BF16)
    mine = spread_out(rows, NEAR).reshape(-1, 128)
    mine, pool_grad = lax.optimization_barrier((mine, pool_grad))
    other = lax.ppermute(mine, "core", swap)
    skip_grad = finish(skip, pool_grad)
    scale = 1.0 / math.sqrt(counts.shape[0] * slots * BX * BY * BZ)
    dec_sum, deep_sum, up_sum, down_sum = pl.pallas_call(
        lambda *refs: unpack_kernel(*refs, scale=scale),
        out_shape=[
            jax.ShapeDtypeStruct((9, C0, C0), F32),
            jax.ShapeDtypeStruct((27, C1, C1), F32),
            jax.ShapeDtypeStruct((C0, C1), F32),
            jax.ShapeDtypeStruct((C0, C1), F32),
        ],
        compiler_params=pltpu.CompilerParams(vmem_limit_bytes=32 * 1024 * 1024),
        name="unpack",
    )(mine, other)
    return skip_grad, dec_sum, deep_sum, up_sum.T, down_sum


def build(fine):
    spec = P(READER, None, None, None)
    return jax.shard_map(
        per_device,
        mesh=fine,
        in_specs=(spec, spec, spec, spec, P(), P(), P(), P(), P()),
        out_specs=(P(READER, "xh", None, None), P(), P(), P(), P()),
        check_vma=False,
    )


def solution(mesh):
    return build(Mesh(mesh.devices.reshape(4, 2, 2, 4, 2, 2), AXES))
```

```python
import math

import jax
import jax.numpy as jnp
from jax import lax
from jax.experimental import pallas as pl
from jax.experimental.pallas import tpu as pltpu
from jax.sharding import Mesh, PartitionSpec as P

C0 = 64
C1 = 128
BX = 16
BY = 16
BZ = 8
F32 = jnp.float32
BF16 = jnp.bfloat16

AXES = ("zh", "zl", "xl", "y", "core", "xh")
READER = ("zh", "zl", "xl", "y", "core")
NEAR = ("zl", "xl", "y", "xh")
FAR = "zh"
AHEAD = 2
UNITS = 16


def cat(parts, axis):
    return parts[0] if len(parts) == 1 else jnp.concatenate(parts, axis=axis)


def lanes(index, width=128):
    return slice(index * width, (index + 1) * width)


def shift_rows(value, distance, keep):
    rows = value.shape[0]
    return jnp.where(keep, pltpu.roll(value, distance % rows, 0), F32(0.0))


def dot(lhs, rhs):
    return jnp.dot(lhs, rhs, preferred_element_type=F32)


def unit_of(dyi, dzi):
    first = 9 * dzi + 3 * dyi
    return (0, first) if first < 15 else (1, first - 15)


def work_kernel(
    counts_ref, grad_hbm, out_hbm, deep_hbm, pooled_hbm, wdec_hbm, wdeep_hbm, wup_hbm, wdown_hbm,
    skip_hbm, pool_grad_ref, mine_ref, other_ref,
    grad_ref, out_ref, deep_ref, pooled_ref, wdec_ref, wdeep_ref, wup_ref, wdown_ref, skip_ref,
    shifted, turned, toeplitz, spread, total, tile, parts, staged,
    start, rect, grads, pools, coarse, deep_turned, wfwd, wback, up_mat, down_mat,
    in_sems, weight_sems, wdeep_sems, skip_sems, part_sems,
):
    half = lax.axis_index("xh")
    core = lax.axis_index("core")
    count = counts_ref[lax.axis_index(READER)]
    sign = 1 - 2 * half
    steps = grad_ref.shape[0] // 2

    def loads(step):
        two = pl.ds(2 * step, 2)
        return [
            pltpu.make_async_copy(
                source.at[two, pl.ds(first, target.shape[1])], target.at[two], in_sems.at[k, step]
            )
            for k, (source, first, target) in enumerate(
                [
                    (grad_hbm, 5 * half, grad_ref),
                    (out_hbm, 6 * half, out_ref),
                    (deep_hbm, 3 * half, deep_ref),
                    (pooled_hbm, 4 * half, pooled_ref),
                ]
            )
        ]

    def weight_load(step):
        taps = pl.ds(3 * step, 3)
        return pltpu.make_async_copy(wdeep_hbm.at[taps], wdeep_ref.at[taps], wdeep_sems.at[step])

    def skip_store(step):
        two = pl.ds(2 * step, 2)
        return pltpu.make_async_copy(skip_ref.at[two], skip_hbm.at[two], skip_sems.at[step])

    weights = [
        pltpu.make_async_copy(source, target, weight_sems.at[k])
        for k, (source, target) in enumerate(
            [(wdec_hbm, wdec_ref), (wup_hbm, wup_ref), (wdown_hbm, wdown_ref)]
        )
    ]
    def load_turn(turn):
        for k in range(AHEAD):
            for copy in loads(AHEAD * turn + k):
                copy.start()
            weight_load(AHEAD * turn + k).start()

    for copy in weights:
        copy.start()
    load_turn(0)
    weight_load(8).start()
    for copy in weights:
        copy.wait()

    def prepare():
        tile[...] = jnp.zeros_like(tile)
        low_lane = lax.broadcasted_iota(jnp.int32, (64, 128), 1) < 64
        backs = []
        for tap in range(9):
            tile[:64, :64] = wdec_ref[tap].astype(F32)
            upper = jnp.where(low_lane, tile[:64], F32(0.0))
            backs.append(cat([upper, pltpu.roll(upper, 64, 1)], 0).T.astype(BF16))
            turned_pair = backs[tap]
            parts[0, tap, :64] = turned_pair[:64].astype(F32)
            parts[0, tap, 64:] = turned_pair[64:].astype(F32)
        for w in range(4):
            for dyi in range(3):
                for xi in range(2):
                    dxf = 1 + xi - w
                    if abs(dxf) <= 1:
                        block = parts[0, 3 * (dxf * sign + 1) + dyi].astype(BF16)
                    else:
                        block = jnp.zeros((128, 128), BF16)
                    toeplitz[lanes(3 * w + dyi), lanes(xi)] = block
        total[...] = jnp.zeros_like(total)
        parts[1, UNITS - 1] = jnp.zeros((128, 128), F32)
        for dyi in range(3):
            for b in range(2):
                for buf in range(AHEAD):
                    shifted[buf, dyi, b, 0] = jnp.zeros((BY, 512), BF16)
            rect[dyi, 0] = jnp.zeros((128, 512), BF16)
            grads[dyi, 0] = jnp.zeros((128, 512), BF16)
        for buf in range(AHEAD):
            turned[buf, 0] = jnp.zeros((128, 128), BF16)
        for z in range(4):
            deep_turned[0, z] = jnp.zeros((128, 128), BF16)
        up_mat[...] = jnp.zeros_like(up_mat)
        down_mat[...] = jnp.zeros_like(down_mat)
        down = wdown_ref[...].astype(F32)
        down_t = cat([down, down], 0).T.astype(BF16)
        for z in range(4):
            up_mat[lanes(z, 64), lanes(z)] = wup_ref[...]
            down_mat[lanes(z), lanes(z)] = down_t

    def deep_weights(step):
        group = 3 * ((step // 3 - 1) * sign + 1) + step % 3
        zero = jnp.zeros((128, 128), BF16)
        plain = [wdeep_ref[3 * step + k] for k in range(3)]
        flipped = [value.T for value in plain]
        for zi in range(3):
            rows = pl.ds(pl.multiple_of((group * 3 + zi) * 128, 128), 128)
            for g in range(2):
                for zo in range(2):
                    dz = (zi + g) - (zo + 2 * g)
                    wfwd[g, rows, lanes(zo)] = plain[dz + 1] if abs(dz) <= 1 else zero
                    wback[g, rows, lanes(zo)] = flipped[1 - dz] if abs(dz) <= 1 else zero

    def build(step, buf):
        deep_weights(step)
        row_id = lax.broadcasted_iota(jnp.int32, (BY, 512), 0)
        not_first = row_id > 0
        not_last = row_id < BY - 1
        deep_first = row_id % 8 > 0
        deep_last = row_id % 8 < 7
        rows = pl.ds(pl.multiple_of(step * 16, 16), 16)
        for b in range(2):
            slot = 2 * step + b
            live = slot < count
            for i in range(11):
                value = grad_ref[slot, half * 10 + sign * i].astype(F32)
                value = jnp.where(live, value, F32(0.0))
                shifted[buf, 0, b, i + 1] = shift_rows(value, -1, not_last).astype(BF16)
                shifted[buf, 1, b, i + 1] = value.astype(BF16)
                shifted[buf, 2, b, i + 1] = shift_rows(value, 1, not_first).astype(BF16)
        for i in range(9):
            tiles = []
            for b in range(2):
                row = out_ref[2 * step + b, half * 9 + sign * i]
                row = jnp.maximum(row, jnp.zeros_like(row))
                tiles += [row[:, lanes(z)] for z in range(4)]
            turned[buf, i + 1] = cat(tiles, 0).T
        for i in range(5):
            source = half * 4 + sign * i
            value = cat([deep_ref[2 * step + b, source].astype(F32) for b in range(2)], 0)
            start[i, rows] = value.astype(BF16)
            value = jnp.maximum(value, F32(0.0))
            rect[0, i + 1, rows] = shift_rows(value, 1, deep_first).astype(BF16)
            rect[1, i + 1, rows] = value.astype(BF16)
            rect[2, i + 1, rows] = shift_rows(value, -1, deep_last).astype(BF16)
            if i < 4:
                source = half * 3 + sign * i
                value = cat([pooled_ref[2 * step + b, source].astype(F32) for b in range(2)], 0)
                pools[i, rows] = value.astype(BF16)

    def back(buf):
        lhs = cat(
            [
                cat(
                    [
                        shifted[buf, dyi, b, 2 * xp + w, :, lanes(z)]
                        for b in range(2)
                        for xp in range(5)
                        for z in range(4)
                    ],
                    0,
                )
                for w in range(4)
                for dyi in range(3)
            ],
            1,
        )
        return dot(lhs, toeplitz[...])

    def outer(buf):
        lhs = cat([cat([turned[buf, i + dxi] for i in range(8)], 1) for dxi in range(3)], 0)
        rhs = cat(
            [
                cat([shifted[buf, dyi, b, i + 1, :, lanes(z)] for dyi in range(3)], 1)
                for i in range(8)
                for b in range(2)
                for z in range(4)
            ],
            0,
        )
        return dot(lhs, rhs)

    def settle(step, buf, backed):
        rows = pl.ds(pl.multiple_of(step * 16, 16), 16)
        low_lane = lax.broadcasted_iota(jnp.int32, (8, 128), 1) < 64
        for xp in range(5):
            pooled = []
            for b in range(2):
                both = []
                for xi in range(2):
                    i = 2 * xp + xi
                    base = (b * 5 + xp) * 64
                    conv = cat(
                        [backed[base + 16 * z : base + 16 * z + 16, lanes(xi)] for z in range(4)], 1
                    )
                    gate = out_ref[2 * step + b, half * 9 + sign * i].astype(F32) > 0
                    value = shifted[buf, 1, b, i + 1].astype(F32) + jnp.where(gate, conv, F32(0.0))
                    value = value.astype(BF16)
                    if i < 8:
                        skip_ref[2 * step + b, half * 7 + sign * i] = value
                    both.append(value.astype(F32))
                cell = both[0] + both[1]
                quads = []
                for z in range(4):
                    piece = cell[:, lanes(z)]
                    place = ((buf * 5 + xp) * 2 + b) * 4 + z
                    spread[place] = piece + pltpu.roll(piece, 64, 1)
                    even = spread[place, pl.ds(0, 8, stride=2), :]
                    quads.append(even + spread[place, pl.ds(1, 8, stride=2), :])
                pooled.append(
                    cat(
                        [jnp.where(low_lane, quads[2 * k], quads[2 * k + 1]) for k in range(2)], 1
                    )
                )
            coarse[xp, rows] = cat(pooled, 0).astype(BF16)

    def shallow(turn, carry):
        mine = [AHEAD * turn + k for k in range(AHEAD)]

        @pl.when(turn + 1 < steps // AHEAD)
        def _():
            load_turn(turn + 1)

        for step in mine:
            for copy in loads(step):
                copy.wait()
            weight_load(step).wait()
        outers = []
        for buf, step in enumerate(mine):
            build(step, buf)
        for buf, step in enumerate(mine):
            backed = back(buf)
            outers.append(outer(buf))
            settle(step, buf, backed)
        total[...] += sum(outers)
        for step in mine:
            skip_store(step).start()
        return carry

    def deep():
        weight_load(8).wait()
        deep_weights(8)
        row_id = lax.broadcasted_iota(jnp.int32, (128, 512), 0) % 8
        not_first = row_id > 0
        not_last = row_id < 7

        grad = dot(cat([coarse[i] for i in range(5)], 0), up_mat[...])
        for i in range(5):
            value = grad[lanes(i)].astype(BF16).astype(F32)
            grads[0, i + 1] = shift_rows(value, -1, not_last).astype(BF16)
            grads[1, i + 1] = value.astype(BF16)
            grads[2, i + 1] = shift_rows(value, 1, not_first).astype(BF16)
            for z in range(4):
                deep_turned[i + 1, z] = rect[1, i + 1, :, lanes(z)].T

        outs = []
        for g in range(2):
            wide = slice(g * 128, g * 128 + 384)
            lhs = cat(
                [
                    cat([rect[dyi, i + dxi, :, wide] for i in range(4)], 0)
                    for dxi in range(3)
                    for dyi in range(3)
                ],
                1,
            )
            conv = dot(lhs, wfwd[g])
            first = cat([start[i, :, lanes(g, 256)] for i in range(4)], 0).astype(F32)
            outs.append((first + conv).astype(BF16))
        coarse_t = cat([coarse[i].T for i in range(4)], 1)
        full = dot(coarse_t, cat(outs, 1))
        parts[0, UNITS - 1, :64] = sum(full[lanes(z, 64), lanes(z)] for z in range(4))

        for dzi in range(3):
            dz = dzi - 1
            levels = [z for z in range(4) if 0 <= z + dz < 4]
            lhs = cat(
                [
                    cat([deep_turned[i + dxi, z + dz] for z in levels for i in range(4)], 1)
                    for dxi in range(3)
                ],
                0,
            )
            rhs = cat(
                [
                    cat([grads[dyi, i + 1, :, lanes(z)] for dyi in range(3)], 1)
                    for z in levels
                    for i in range(4)
                ],
                0,
            )
            part = dot(lhs, rhs)
            for dyi in range(3):
                side, first = unit_of(dyi, dzi)
                for dxi in range(3):
                    parts[side, first + (dxi - 1) * sign + 1] = part[lanes(dxi), lanes(dyi)]

        low = lax.broadcasted_iota(jnp.int32, (64, 128), 1) < 64
        low_half = lax.broadcasted_iota(jnp.int32, (32, 128), 1) < 64
        for dxi in range(3):
            for dyi in range(3):
                block = total[lanes(dxi), lanes(dyi)]
                turned_lanes = pltpu.roll(block, 64, 1)
                summed = jnp.where(
                    low, block[:64] + turned_lanes[64:], block[64:] + turned_lanes[:64]
                )
                summed = jnp.where(low_half, summed[:32], summed[32:])
                row = pl.multiple_of(((dxi - 1) * sign + 1) * 32, 32)
                parts[1, 12 + dyi, pl.ds(row, 32)] = summed
        for dyi in range(3):
            parts[1, 12 + dyi, 96:] = jnp.zeros((32, 128), F32)
        stage_parts(0, UNITS - 1)

        outs = []
        for g in range(2):
            wide = slice(g * 128, g * 128 + 384)
            lhs = cat(
                [
                    cat([grads[dyi, i + 2 - dxi, :, wide] for i in range(4)], 0)
                    for dxi in range(3)
                    for dyi in range(3)
                ],
                1,
            )
            conv = dot(lhs, wback[g])
            first = cat([start[i, :, lanes(g, 256)] for i in range(4)], 0).astype(F32)
            base = cat([grads[1, i + 1, :, lanes(g, 256)] for i in range(4)], 0).astype(F32)
            outs.append((base + jnp.where(first > 0, conv, F32(0.0))).astype(BF16))
        input_grad = cat(outs, 1)
        full = dot(cat([pools[i].T for i in range(4)], 1), input_grad)
        parts[0, UNITS - 1, 64:] = sum(full[lanes(z, 64), lanes(z)] for z in range(4))
        stage_parts(UNITS - 1, 1)
        pool_grad = dot(input_grad, down_mat[...]).astype(BF16)
        for i in range(4):
            pool_grad_ref[i] = pool_grad[lanes(i)]

    def stage_parts(first, number):
        for unit in range(first, first + number):
            staged[unit] = parts[1 - core, unit].astype(BF16)
        for copy in part_copies(first, number):
            copy.start()

    def part_copies(first, number):
        units = pl.ds(first, number)
        late = 0 if first == 0 else 2
        return [
            pltpu.make_async_copy(staged.at[units], other_ref.at[units], part_sems.at[late]),
            pltpu.make_async_copy(parts.at[core, units], mine_ref.at[units], part_sems.at[late + 1]),
        ]

    prepare()
    lax.fori_loop(0, steps // AHEAD, shallow, 0)
    deep()
    for k in range(steps):
        skip_store(k).wait()
    for copy in part_copies(0, UNITS - 1) + part_copies(UNITS - 1, 1):
        copy.wait()


def finish_kernel(skip_ref, pool_ref, done_ref, spread):
    half = lax.axis_index("xh")
    sign = 1 - 2 * half
    for i in range(4):
        for p in range(2):
            coarse = pool_ref[i, 16 * p : 16 * p + 16].astype(F32) * F32(0.125)
            for b in range(2):
                value = coarse[8 * b : 8 * b + 8]
                wide = []
                for z in range(4):
                    slot = ((i * 2 + p) * 2 + b) * 4 + z
                    spread[slot, pl.ds(0, 8, stride=2), :] = value[:, lanes(z)]
                    spread[slot, pl.ds(1, 8, stride=2), :] = value[:, lanes(z)]
                    wide.append(spread[slot])
                wide = cat(wide, 1)
                for xi in range(2):
                    row = half * 7 + sign * (2 * i + xi)
                    value_in = skip_ref[2 * p + b, row].astype(F32)
                    done_ref[2 * p + b, row] = (value_in + wide).astype(BF16)


def unpack_kernel(mine_ref, other_ref, dec_ref, deep_ref, up_ref, down_ref, *, scale):
    first_half = lax.axis_index("core") == 0

    def unit(side, index):
        rows = lanes(index)
        mine = mine_ref[rows].astype(F32)
        other = other_ref[rows].astype(F32)
        return jnp.where(first_half, *((mine, other) if side == 0 else (other, mine))) * F32(scale)

    for dyi in range(3):
        for dzi in range(3):
            side, first = unit_of(dyi, dzi)
            for dxi in range(3):
                deep_ref[9 * dxi + 3 * dyi + dzi] = unit(side, first + dxi)
        block = unit(1, 12 + dyi)
        for dxi in range(3):
            piece = block[lanes(dxi, 32)]
            dec_ref[3 * dxi + dyi, :32] = piece[:, :64]
            dec_ref[3 * dxi + dyi, 32:] = pltpu.roll(piece, 64, 1)[:, :64]
    block = unit(0, UNITS - 1)
    up_ref[...] = block[:64]
    down_ref[...] = block[64:]


def work(counts, dec_input, out_cotangent, pooled_skip, deep_input, dec_weight, deep_weight, up_weight, down_weight):
    slots = dec_input.shape[0]
    steps = slots // 2
    anywhere = pl.BlockSpec(memory_space=pl.ANY)
    return pl.pallas_call(
        work_kernel,
        in_specs=[pl.BlockSpec(memory_space=pltpu.SMEM)] + [anywhere] * 8,
        out_specs=[anywhere, pl.BlockSpec(memory_space=pltpu.VMEM), anywhere, anywhere],
        scratch_shapes=[
            pltpu.VMEM((slots, 11, BY, 512), BF16),
            pltpu.VMEM((slots, 10, BY, 512), BF16),
            pltpu.VMEM((slots, 5, 8, 512), BF16),
            pltpu.VMEM((slots, 4, 8, 256), BF16),
            pltpu.VMEM((9, 64, 64), BF16),
            pltpu.VMEM((27, 128, 128), BF16),
            pltpu.VMEM((64, 128), BF16),
            pltpu.VMEM((64, 128), BF16),
            pltpu.VMEM((slots, 8, BY, 512), BF16),
            pltpu.VMEM((AHEAD, 3, 2, 12, BY, 512), BF16),
            pltpu.VMEM((AHEAD, 10, 128, 128), BF16),
            pltpu.VMEM((1536, 256), BF16),
            pltpu.VMEM((40 * AHEAD, BY, 128), F32),
            pltpu.VMEM((384, 384), F32),
            pltpu.VMEM((128, 128), F32),
            pltpu.VMEM((2, UNITS, 128, 128), F32),
            pltpu.VMEM((UNITS, 128, 128), BF16),
            pltpu.VMEM((5, 128, 512), BF16),
            pltpu.VMEM((3, 6, 128, 512), BF16),
            pltpu.VMEM((3, 6, 128, 512), BF16),
            pltpu.VMEM((4, 128, 256), BF16),
            pltpu.VMEM((5, 128, 256), BF16),
            pltpu.VMEM((6, 4, 128, 128), BF16),
            pltpu.VMEM((2, 3456, 256), BF16),
            pltpu.VMEM((2, 3456, 256), BF16),
            pltpu.VMEM((256, 512), BF16),
            pltpu.VMEM((512, 512), BF16),
            pltpu.SemaphoreType.DMA((4, steps)),
            pltpu.SemaphoreType.DMA((3,)),
            pltpu.SemaphoreType.DMA((9,)),
            pltpu.SemaphoreType.DMA((steps,)),
            pltpu.SemaphoreType.DMA((4,)),
        ],
        out_shape=[
            jax.ShapeDtypeStruct((slots, 8, BY, 512), BF16),
            jax.ShapeDtypeStruct((4, 8 * slots, 512), BF16),
            jax.ShapeDtypeStruct((UNITS, 128, 128), F32),
            jax.ShapeDtypeStruct((UNITS, 128, 128), BF16),
        ],
        compiler_params=pltpu.CompilerParams(vmem_limit_bytes=60 * 1024 * 1024),
        name="work",
    )(counts, out_cotangent, dec_input, deep_input, pooled_skip, dec_weight, deep_weight, up_weight.T, down_weight)


def finish(skip, pool_grad):
    slots = skip.shape[0]
    blocks = pl.BlockSpec((4, 8, BY, 512), lambda s: (s, 0, 0, 0))
    return pl.pallas_call(
        finish_kernel,
        grid=(slots // 4,),
        in_specs=[blocks, pl.BlockSpec((4, 32, 512), lambda s: (0, s, 0))],
        out_specs=blocks,
        scratch_shapes=[pltpu.VMEM((64, BY, 128), F32)],
        out_shape=jax.ShapeDtypeStruct(skip.shape, BF16),
        compiler_params=pltpu.CompilerParams(vmem_limit_bytes=12 * 1024 * 1024),
        cost_estimate=pl.CostEstimate(flops=1 << 20, bytes_accessed=1 << 23, transcendentals=0),
        name="finish",
    )(skip, pool_grad)


def scatter_sum(rows, axes):
    split = rows.reshape(lax.axis_size(axes), -1, 128)
    split = lax.all_to_all(split, axes, 0, 0, tiled=True)
    return split.astype(F32).sum(axis=0)


def spread_out(rows, axes):
    copies = jnp.broadcast_to(rows[None], (lax.axis_size(axes),) + rows.shape)
    return lax.all_to_all(copies, axes, 0, 0, tiled=True)


def per_device(
    dec_input, out_cotangent, pooled_skip, deep_input,
    dec_weight, deep_weight, up_weight, down_weight, counts,
):
    slots = dec_input.shape[0]
    swap = [(0, 1), (1, 0)]
    skip, pool_grad, mine, other = work(
        counts, dec_input, out_cotangent, pooled_skip, deep_input,
        dec_weight, deep_weight, up_weight, down_weight,
    )
    other = lax.ppermute(other, "core", swap)
    rows = (mine + other.astype(F32)).astype(BF16).reshape(-1, 128)
    rows = scatter_sum(rows, NEAR)
    rows = spread_out(rows, FAR).sum(axis=0).astype(BF16)
    mine = spread_out(rows, NEAR).reshape(-1, 128)
    mine, pool_grad = lax.optimization_barrier((mine, pool_grad))
    other = lax.ppermute(mine, "core", swap)
    skip_grad = finish(skip, pool_grad)
    scale = 1.0 / math.sqrt(counts.shape[0] * slots * BX * BY * BZ)
    dec_sum, deep_sum, up_sum, down_sum = pl.pallas_call(
        lambda *refs: unpack_kernel(*refs, scale=scale),
        out_shape=[
            jax.ShapeDtypeStruct((9, C0, C0), F32),
            jax.ShapeDtypeStruct((27, C1, C1), F32),
            jax.ShapeDtypeStruct((C0, C1), F32),
            jax.ShapeDtypeStruct((C0, C1), F32),
        ],
        compiler_params=pltpu.CompilerParams(vmem_limit_bytes=32 * 1024 * 1024),
        name="unpack",
    )(mine, other)
    return skip_grad, dec_sum, deep_sum, up_sum.T, down_sum


def build(fine):
    spec = P(READER, None, None, None)
    return jax.shard_map(
        per_device,
        mesh=fine,
        in_specs=(spec, spec, spec, spec, P(), P(), P(), P(), P()),
        out_specs=(P(READER, "xh", None, None), P(), P(), P(), P()),
        check_vma=False,
    )


def solution(mesh):
    return build(Mesh(mesh.devices.reshape(4, 2, 2, 4, 2, 2), AXES))
```
